32 devices in a mesh: dp: 4 (over y, core), cell: 8 (over z, x).
Axes of the slice: x: 2, y: 2, z: 4, core: 2. Of those that a mesh axis runs over, the one named last changes fastest.
Arguments:
- sensitivity: bfloat16 [512, 50176], P('dp', 'cell'), may hold values from -0.078125 to 0.078125
- direction: bfloat16 [16, 50176], P(None, 'cell'), may hold values from -6 to 6
- depth_weight: float32 [50176], P('cell'), may hold values from 0.3 to 3
- counts: int32 [8], P('cell'), may hold values from 4704 to 6272, as said below
- send_lists: int32 [8, 2, 128], P('cell'), may hold values from 0 to 6271, as said below
- neighbours: int32 [6, 50176], P(None, 'cell'), may hold values from 0 to 6528, as said below
Outputs:
- product: float32 [16, 50176], P(None, 'cell')
The draws below stay inside these ranges and needn't reach their ends.
Inputs may be any that keep to these rules, and one draw needn't show every extreme that they name: `counts`: every partition has at least 4704 live cells; some partition is full in every draw. `send_lists`: entries are local indices of live cells of their own partition. `neighbours`: entries below 6272 are live local cells that differ from the cell's own local index by at most 64; 6272 to 6527 name received rim cells; 6528 is an absent face; padded slots hold only absent faces.
All inputs are finite; a program needn't handle non-finite values.
Results may differ from the reference program's by a relative error of at most 0.0008.
Values sent between devices are 32-bit elements; how exact they have to be, the bound alone decides.
A program may use at most 64 MiB of HBM per device.

```python
import math
import jax
import jax.numpy as jnp
from jax import lax

C_DEV = 6272
NV = 16
RIM = 128
K = 6
NDATA = 512
NPART = 8
NCELLS = 50176


def part_counts(key):
    base = jax.random.fold_in(key, 11)
    drawn = jax.random.randint(base, (NPART,), 3 * C_DEV // 4, C_DEV + 1)
    full = jax.random.randint(jax.random.fold_in(base, 1), (), 0, NPART)
    return (jnp.where(jnp.arange(NPART) == full, C_DEV, drawn).astype(jnp.int32), full)


def draw_counts(key, part):
    sizes, full = part_counts(key)
    return sizes


def draw_send_lists(key, part):
    sizes, full = part_counts(key)
    raw = jax.random.randint(jax.random.fold_in(key, 22), (NPART, 2, RIM), 0, 1 << 20)
    lists = (raw % sizes[:, None, None]).astype(jnp.int32)
    rows = jnp.arange(NPART, dtype=jnp.int32)[:, None, None]
    sides = jnp.arange(2, dtype=jnp.int32)[None, :, None]
    spots = jnp.arange(RIM, dtype=jnp.int32)[None, None, :]
    first = (rows == full) & (spots == 0)
    lists = jnp.where(first & (sides == 0), C_DEV - 1, lists)
    lists = jnp.where(first & (sides == 1), 0, lists)
    return lists.astype(jnp.int32)


def draw_neighbours(key, part):
    sizes, full = part_counts(key)
    base = jax.random.fold_in(key, 33)
    kinds = jax.random.randint(jax.random.fold_in(base, 1), (K, NPART, C_DEV), 0, 8)
    offset = jax.random.randint(jax.random.fold_in(base, 2), (K, NPART, C_DEV), -64, 65)
    rimpick = jax.random.randint(jax.random.fold_in(base, 3), (K, NPART, C_DEV), 0, 2 * RIM)
    position = jnp.arange(C_DEV, dtype=jnp.int32)[None, None, :]
    limit = sizes[None, :, None]
    nearby = jnp.clip(position + offset, 0, limit - 1)
    sentinel = C_DEV + 2 * RIM
    chosen = jnp.where(kinds < 5, nearby, jnp.where(kinds == 5, C_DEV + rimpick, sentinel))
    chosen = jnp.where(position < limit, chosen, sentinel)
    return chosen.reshape(K, NPART * C_DEV).astype(jnp.int32)


def shard_levels(rng, dims, shards, least, high):
    factor_of = 1.0
    for dim, shards_of in shards:
        steps = jax.random.uniform(jax.random.fold_in(jax.random.fold_in(rng, 6), dim), (shards_of,), jnp.float32, least / len(shards), high / len(shards))
        factor_of = factor_of * jnp.repeat(jnp.exp(steps), dims[dim] // shards_of).reshape((-1,) + (1,) * (len(dims) - 1 - dim))
    return factor_of


def normal_values(key, shape, scale, most, shards=(), held_as=jnp.bfloat16):
    level = shard_levels(key, shape, shards, -0.22, 0.18) if shards else 1.0
    values = jax.random.normal(key, shape, jnp.float32) * scale * level
    return jnp.minimum(jnp.maximum(values, -most), most).astype(held_as)


def setup_inputs(seed: int = 0) -> dict:
    streams_of = jax.random.split(jax.random.key(seed), 7)
    sensitivity = normal_values(streams_of[0], (NDATA, NCELLS), ((NCELLS * NDATA) ** 0.5) ** -0.5, 0.078125, ((0, 4), (1, 8)))
    direction = normal_values(streams_of[1], (NV, NCELLS), 1.0, 6.0, ((1, 8),))
    depth_weight = jnp.clip(jnp.exp(math.log(3.0) - 2.3025851 * jax.random.uniform(streams_of[2], (NCELLS,), jnp.float32) ** shard_levels(streams_of[2], (NCELLS,), ((0, 8),), -0.2, 0.2)), 0.3, 3.0)
    counts = draw_counts(jax.random.fold_in(streams_of[6], 71), 0)
    send_lists = draw_send_lists(jax.random.fold_in(streams_of[6], 71), 0)
    neighbours = draw_neighbours(jax.random.fold_in(streams_of[6], 71), 0)
    return {"sensitivity": sensitivity, "direction": direction, "depth_weight": depth_weight, "counts": counts, "send_lists": send_lists, "neighbours": neighbours}


def reference(sensitivity, direction, depth_weight, counts, send_lists, neighbours):
    slots = jnp.arange(NCELLS, dtype=jnp.int32)
    local = slots % C_DEV
    owner = slots // C_DEV
    live = local < counts[owner]
    masked = jnp.where(live[None, :], direction, jnp.zeros_like(direction)).astype(jnp.bfloat16)
    predicted = lax.dot_general(masked, sensitivity, (((1,), (1,)), ((), ())), preferred_element_type=jnp.float32)
    rounded = predicted.astype(jnp.bfloat16)
    remainder = (predicted - rounded.astype(jnp.float32)).astype(jnp.bfloat16)
    stacked = jnp.concatenate([rounded, remainder], axis=0)
    both = jnp.dot(stacked, sensitivity, preferred_element_type=jnp.float32)
    misfit = both[:NV] + both[NV:]
    weight = jnp.where(live, depth_weight, jnp.float32(0.0))
    values = jnp.concatenate([masked.astype(jnp.float32), weight[None, :]], axis=0)
    blocks = values.reshape(NV + 1, NPART, C_DEV)
    index = jnp.broadcast_to(send_lists.reshape(1, NPART, 2 * RIM), (NV + 1, NPART, 2 * RIM))
    sent = jnp.take_along_axis(blocks, index, axis=2)
    lower = sent[:, :, :RIM]
    upper = sent[:, :, RIM:]
    zero_rim = jnp.zeros((NV + 1, 1, RIM), jnp.float32)
    prev_upper = jnp.concatenate([zero_rim, upper[:, :-1]], axis=1)
    next_lower = jnp.concatenate([lower[:, 1:], zero_rim], axis=1)
    extended = jnp.concatenate([blocks, prev_upper, next_lower, jnp.zeros((NV + 1, NPART, 1), jnp.float32)], axis=2)
    width = extended.shape[2]
    faces = neighbours.reshape(K, NPART, C_DEV)
    big_ext = jnp.broadcast_to(extended[:, None], (NV + 1, K, NPART, width))
    big_idx = jnp.broadcast_to(faces[None], (NV + 1, K, NPART, C_DEV))
    found = jnp.take_along_axis(big_ext, big_idx, axis=3)
    own_p = blocks[:NV]
    own_w = blocks[NV]
    near_w = found[NV]
    near_p = found[:NV]
    coupling = jnp.sum(near_w[None] * (own_p[:, None] - near_p), axis=1)
    smooth = own_w[None] * own_w[None] * own_p + own_w[None] * coupling
    total = misfit + 0.5 * smooth.reshape(NV, NCELLS)
    return jnp.where(live[None, :], total, jnp.float32(0.0))
```

```python
import functools

import jax
import jax.numpy as jnp
from jax import lax
from jax.experimental import pallas as pl
from jax.experimental.pallas import tpu as pltpu
from jax.sharding import PartitionSpec as P

LANES = 128
REACH = 64
MESH = pl.DeviceIdType.MESH
F32 = jnp.float32
BF16 = jnp.bfloat16


def pick_chunk(blocks):
    for size in (5, 6, 4, 3, 2):
        if blocks % size == 0:
            return size
    return 1


def split2(value):
    hi = value.astype(BF16)
    return hi, (value - hi.astype(F32)).astype(BF16)


def stack_rows(weighted, weight):
    hi, lo = split2(weighted)
    w_hi, w_lo = split2(weight)
    shape = (16, weight.shape[1])
    row = lax.broadcasted_iota(jnp.int32, shape, 0)
    wide_hi = jnp.broadcast_to(w_hi.astype(F32), shape)
    wide_lo = jnp.broadcast_to(w_lo.astype(F32), shape)
    tail = jnp.where(row == 0, wide_hi, jnp.where(row == 1, wide_lo, F32(0.0)))
    return jnp.concatenate([hi, lo, tail.astype(BF16)], axis=0)


def count_hits(columns, rows):
    target = lax.broadcasted_iota(jnp.int32, (rows, columns.shape[1]), 0)
    hits = jnp.zeros((rows, columns.shape[1]), F32)
    for k in range(columns.shape[0]):
        hits = hits + jnp.where(columns[k : k + 1, :] == target, F32(1.0), F32(0.0))
    return hits.astype(BF16)


def kernel(
    n, n_dp, sens_hbm, dir_hbm, w_ref, cnt_ref, send_ref, nbr_hbm, out_ref,
    s_v, d_v, n_v, g, pmf, wrow, preds, rim_out, rim_in, acc, sm, ms, rs, ys,
    in_sem, bar_pred_s, bar_pred_r, rim_s, rim_r, rs_s, rs_r, y_s, y_r, fin_s, fin_r,
):
    nvec, slots = d_v.shape
    nb = slots // LANES
    half = (nb + 1) // 2
    swap_end = nb - half
    chunk = pick_chunk(half)
    n_chunks = half // chunk
    n_y = n_dp // 2
    piece = (half + n_y - 1) // n_y
    rim = rim_out.shape[2]

    cell = lax.axis_index("cell")
    dp = lax.axis_index("dp")
    y = dp // 2
    core = dp % 2
    sibling = y * 2 + 1 - core

    c_s = pltpu.make_async_copy(sens_hbm, s_v, in_sem.at[0])
    c_d = pltpu.make_async_copy(dir_hbm, d_v, in_sem.at[1])
    c_n = pltpu.make_async_copy(nbr_hbm, n_v, in_sem.at[2])
    c_d.start()
    c_s.start()
    c_n.start()

    barrier = pltpu.get_barrier_semaphore()
    for k in range(1, n):
        pl.semaphore_signal(barrier, inc=1, device_id={"cell": (cell + k) % n}, device_id_type=MESH)
    pl.semaphore_signal(barrier, inc=1, device_id={"dp": sibling}, device_id_type=MESH)
    for k in range(1, n_y):
        pl.semaphore_signal(
            barrier, inc=1, device_id={"dp": ((y + k) % n_y) * 2 + core}, device_id_type=MESH
        )

    count = cnt_ref[0]
    live = lax.broadcasted_iota(jnp.int32, (1, slots), 1) < count
    c_d.wait()
    masked = jnp.where(live, d_v[...].astype(F32), F32(0.0))
    pmf[...] = masked
    weight = jnp.where(live, w_ref[...], F32(0.0))
    wrow[...] = weight
    c_s.wait()
    preds[cell] = lax.dot_general(
        masked.astype(BF16), s_v[...], (((1,), (1,)), ((), ())), preferred_element_type=F32
    )

    pl.semaphore_wait(barrier, n + n_y - 1)
    sends = []
    for k in range(1, n):
        copy = pltpu.make_async_remote_copy(
            src_ref=preds.at[cell], dst_ref=preds.at[cell],
            send_sem=bar_pred_s.at[k], recv_sem=bar_pred_r.at[cell],
            device_id={"cell": (cell + k) % n}, device_id_type=MESH,
        )
        copy.start()
        sends.append(copy)

    pad = jnp.zeros((nvec, LANES), F32)
    wide = jnp.concatenate([masked * weight, pad], axis=1)
    wide_w = jnp.concatenate([weight, pad[:1]], axis=1)
    wide_w = pltpu.roll(jnp.broadcast_to(wide_w, (8, slots + LANES)), REACH, 1)
    g[...] = stack_rows(pltpu.roll(wide, REACH, 1), wide_w[0:1])

    lists = jnp.concatenate([send_ref[0, 0:1, :], send_ref[0, 1:2, :]], axis=1) + REACH
    step = 10 * LANES if (slots + LANES) % (10 * LANES) == 0 else LANES

    def pick(i, total):
        at = pl.multiple_of(i * step, step)
        hits = count_hits(lists - at, step)
        return total + jnp.dot(g[:, pl.ds(at, step)], hits, preferred_element_type=F32)

    picked = lax.fori_loop(
        0, (slots + LANES) // step, pick, jnp.zeros((3 * nvec, 2 * rim), F32)
    )
    for side in range(2):
        part = picked[:, side * rim : (side + 1) * rim]
        rim_out[side, 0:16] = part[0:16] + part[16:32]
        rim_out[side, 16:24] = jnp.broadcast_to(part[32:33] + part[33:34], (8, rim))
    for side in range(2):
        copy = pltpu.make_async_remote_copy(
            src_ref=rim_out.at[side], dst_ref=rim_in.at[1 - side],
            send_sem=rim_s.at[side], recv_sem=rim_r.at[1 - side],
            device_id={"cell": (cell + n - 1 + 2 * side) % n}, device_id_type=MESH,
        )
        copy.start()
        sends.append(copy)

    first_t = jnp.minimum(y * piece, half - piece)
    first_block = first_t + core * (nb - 2 * first_t - piece)
    sm[...] = jnp.zeros_like(sm)
    c_n.wait()

    def near(i, carry):
        at = pl.multiple_of((first_block + i) * LANES, LANES)
        hits = count_hits(n_v[:, pl.ds(at, LANES)] - at + REACH, 2 * LANES)
        acc[i] = jnp.dot(g[:, pl.ds(at, 2 * LANES)], hits, preferred_element_type=F32)
        return carry

    lax.fori_loop(0, piece, near, 0)

    sides = []
    for side in range(2):
        pltpu.make_async_remote_copy(
            src_ref=rim_out.at[side], dst_ref=rim_in.at[side],
            send_sem=rim_s.at[side], recv_sem=rim_r.at[side],
            device_id={"cell": (cell + n - 1 + 2 * side) % n}, device_id_type=MESH,
        ).wait_recv()
        there = cell > 0 if side == 0 else cell < n - 1
        got = jnp.where(there, rim_in[side], F32(0.0))
        sides.append(stack_rows(got[0:16], got[16:17]))
    rim_rows = jnp.concatenate(sides, axis=1)

    def far(i, carry):
        block = first_block + i
        at = pl.multiple_of(block * LANES, LANES)
        hits = count_hits(n_v[:, pl.ds(at, LANES)] - slots, 2 * rim)
        found = acc[i] + jnp.dot(rim_rows, hits, preferred_element_type=F32)
        sum_pw = found[0:16] + found[16:32]
        sum_w = found[32:33] + found[33:34]
        own_p = pmf[:, pl.ds(at, LANES)]
        own_w = wrow[:, pl.ds(at, LANES)]
        smooth = own_w * own_w * own_p + own_w * (own_p * sum_w - sum_pw)
        t = block + core * (nb - 1 - 2 * block)
        mine = jnp.logical_and(t >= y * piece, t < (y + 1) * piece)
        sm[:, pl.ds(at, LANES)] = smooth * jnp.where(mine, F32(0.5), F32(0.0))
        return carry

    lax.fori_loop(0, piece, far, 0)

    for k in range(1, n):
        source = (cell + k) % n
        pltpu.make_async_remote_copy(
            src_ref=preds.at[source], dst_ref=preds.at[source],
            send_sem=bar_pred_s.at[k], recv_sem=bar_pred_r.at[source],
            device_id={"cell": source}, device_id_type=MESH,
        ).wait_recv()
    predicted = preds[0]
    for k in range(1, n):
        predicted = predicted + preds[k]
    stacked = jnp.concatenate(split2(predicted), axis=0)

    def misfit(at):
        both = jnp.dot(stacked, s_v[:, pl.ds(at, chunk * LANES)], preferred_element_type=F32)
        return both[:nvec] + both[nvec:]

    def lanes_at(block):
        return pl.multiple_of(block * LANES, LANES)

    for c in range(n_chunks):
        a, b = c * chunk, (c + 1) * chunk
        ms[c] = misfit(lanes_at((1 - core) * (nb - b) + core * a))
        copy = pltpu.make_async_remote_copy(
            src_ref=ms.at[c], dst_ref=rs.at[c], send_sem=rs_s.at[c], recv_sem=rs_r.at[c],
            device_id={"dp": sibling}, device_id_type=MESH,
        )
        copy.start()
        sends.append(copy)

    for c in range(n_chunks):
        a, b = c * chunk, (c + 1) * chunk
        at = lanes_at(core * (nb - b) + (1 - core) * a)
        own = misfit(at)
        pltpu.make_async_remote_copy(
            src_ref=ms.at[c], dst_ref=rs.at[c], send_sem=rs_s.at[c], recv_sem=rs_r.at[c],
            device_id={"dp": sibling}, device_id_type=MESH,
        ).wait_recv()
        ys[y, c] = (own + rs[c]) + sm[:, pl.ds(at, chunk * LANES)]
        for k in range(1, n_y):
            copy = pltpu.make_async_remote_copy(
                src_ref=ys.at[y, c], dst_ref=ys.at[y, c],
                send_sem=y_s.at[k, c], recv_sem=y_r.at[y, c],
                device_id={"dp": ((y + k) % n_y) * 2 + core}, device_id_type=MESH,
            )
            copy.start()
            sends.append(copy)

    final = []
    for c in range(n_chunks):
        a, b = c * chunk, (c + 1) * chunk
        at = lanes_at(core * (nb - b) + (1 - core) * a)
        for k in range(1, n_y):
            source = (y + k) % n_y
            pltpu.make_async_remote_copy(
                src_ref=ys.at[source, c], dst_ref=ys.at[source, c],
                send_sem=y_s.at[k, c], recv_sem=y_r.at[source, c],
                device_id={"dp": source * 2 + core}, device_id_type=MESH,
            ).wait_recv()
        total = ys[0, c]
        for k in range(1, n_y):
            total = total + ys[k, c]
        place = lax.broadcasted_iota(jnp.int32, (1, chunk * LANES), 1) + at
        out_ref[:, pl.ds(at, chunk * LANES)] = jnp.where(place < count, total, F32(0.0))
        end = min(b, swap_end)
        if end > a:
            width = (end - a) * LANES
            here = lanes_at(core * (nb - end) + (1 - core) * a)
            there = lanes_at((1 - core) * (nb - end) + core * a)
            copy = pltpu.make_async_remote_copy(
                src_ref=out_ref.at[:, pl.ds(here, width)], dst_ref=out_ref.at[:, pl.ds(here, width)],
                send_sem=fin_s.at[c], recv_sem=fin_r.at[c],
                device_id={"dp": sibling}, device_id_type=MESH,
            )
            copy.start()
            sends.append(copy)
            final.append(
                pltpu.make_async_remote_copy(
                    src_ref=out_ref.at[:, pl.ds(there, width)],
                    dst_ref=out_ref.at[:, pl.ds(there, width)],
                    send_sem=fin_s.at[c], recv_sem=fin_r.at[c],
                    device_id={"dp": sibling}, device_id_type=MESH,
                )
            )
    for copy in final:
        copy.wait_recv()
    for copy in sends:
        copy.wait_send()


def on_device(n, n_dp, sensitivity, direction, depth_weight, counts, send_lists, neighbours):
    ndata, slots = sensitivity.shape
    nvec = direction.shape[0]
    faces = neighbours.shape[0]
    rim = send_lists.shape[2]
    nb = slots // LANES
    half = (nb + 1) // 2
    chunk = pick_chunk(half)
    n_chunks = half // chunk
    n_y = n_dp // 2
    piece = (half + n_y - 1) // n_y
    vmem = pl.BlockSpec(memory_space=pltpu.VMEM)
    hbm = pl.BlockSpec(memory_space=pl.ANY)
    dma = pltpu.SemaphoreType.DMA
    return pl.pallas_call(
        functools.partial(kernel, n, n_dp),
        out_shape=jax.ShapeDtypeStruct((nvec, slots), F32),
        in_specs=[hbm, hbm, vmem, pl.BlockSpec(memory_space=pltpu.SMEM), vmem, hbm],
        out_specs=vmem,
        scratch_shapes=[
            pltpu.VMEM((ndata, slots), BF16),
            pltpu.VMEM((nvec, slots), BF16),
            pltpu.VMEM((faces, slots), jnp.int32),
            pltpu.VMEM((3 * nvec, slots + LANES), BF16),
            pltpu.VMEM((nvec, slots), F32),
            pltpu.VMEM((1, slots), F32),
            pltpu.VMEM((n, nvec, ndata), F32),
            pltpu.VMEM((2, nvec + 8, rim), F32),
            pltpu.VMEM((2, nvec + 8, rim), F32),
            pltpu.VMEM((piece, 3 * nvec, LANES), F32),
            pltpu.VMEM((nvec, slots), F32),
            pltpu.VMEM((n_chunks, nvec, chunk * LANES), F32),
            pltpu.VMEM((n_chunks, nvec, chunk * LANES), F32),
            pltpu.VMEM((n_y, n_chunks, nvec, chunk * LANES), F32),
            dma((3,)),
            dma((n,)),
            dma((n,)),
            dma((2,)),
            dma((2,)),
            dma((n_chunks,)),
            dma((n_chunks,)),
            dma((n_y, n_chunks)),
            dma((n_y, n_chunks)),
            dma((n_chunks,)),
            dma((n_chunks,)),
        ],
        compiler_params=pltpu.CompilerParams(
            collective_id=0, has_side_effects=True, vmem_limit_bytes=40 * 1024 * 1024
        ),
    )(sensitivity, direction, depth_weight.reshape(1, slots), counts, send_lists, neighbours)


def solution(mesh):
    placed = (
        P("dp", "cell"),
        P(None, "cell"),
        P("cell"),
        P("cell"),
        P("cell", None, None),
        P(None, "cell"),
    )
    return jax.shard_map(
        functools.partial(on_device, mesh.shape["cell"], mesh.shape["dp"]),
        mesh=mesh, in_specs=placed, out_specs=P(None, "cell"), check_vma=False,
    )
```

```python
import functools

import jax
import jax.numpy as jnp
from jax import lax
from jax.experimental import pallas as pl
from jax.experimental.pallas import tpu as pltpu
from jax.sharding import PartitionSpec as P

LANES = 128
REACH = 64
MESH = pl.DeviceIdType.MESH
F32 = jnp.float32
BF16 = jnp.bfloat16


def pick_chunk(blocks):
    for size in (5, 6, 4, 3, 2):
        if blocks % size == 0:
            return size
    return 1


def split2(value):
    hi = value.astype(BF16)
    return hi, (value - hi.astype(F32)).astype(BF16)


def stack_rows(weighted, weight):
    hi, lo = split2(weighted)
    w_hi, w_lo = split2(weight)
    shape = (16, weight.shape[1])
    row = lax.broadcasted_iota(jnp.int32, shape, 0)
    wide_hi = jnp.broadcast_to(w_hi.astype(F32), shape)
    wide_lo = jnp.broadcast_to(w_lo.astype(F32), shape)
    tail = jnp.where(row == 0, wide_hi, jnp.where(row == 1, wide_lo, F32(0.0)))
    return jnp.concatenate([hi, lo, tail.astype(BF16)], axis=0)


def count_hits(columns, rows):
    narrow = columns.astype(jnp.int16)
    target = lax.broadcasted_iota(jnp.int16, (rows, columns.shape[1]), 0)
    hits = jnp.zeros((rows, columns.shape[1]), BF16)
    for k in range(columns.shape[0]):
        hits = hits + jnp.where(narrow[k : k + 1, :] == target, BF16(1.0), BF16(0.0))
    return hits


def kernel(
    n, n_dp, sens_hbm, dir_hbm, w_hbm, cnt_ref, send_hbm, nbr_hbm, out_ref,
    s_v, d_v, n_v, w_v, l_v, g, pmf, wrow, preds, rim_out, rim_in, acc, sm, ms, rs, ys,
    in_sem, bar_pred_s, bar_pred_r, rim_s, rim_r, rs_s, rs_r, y_s, y_r, fin_s, fin_r,
):
    nvec, slots = d_v.shape
    nb = slots // LANES
    half = (nb + 1) // 2
    swap_end = nb - half
    chunk = pick_chunk(half)
    n_chunks = half // chunk
    n_y = n_dp // 2
    piece = (half + n_y - 1) // n_y
    rim = rim_out.shape[2]

    cell = lax.axis_index("cell")
    dp = lax.axis_index("dp")
    y = dp // 2
    core = dp % 2
    sibling = y * 2 + 1 - core

    c_s = pltpu.make_async_copy(sens_hbm, s_v, in_sem.at[0])
    c_d = pltpu.make_async_copy(dir_hbm, d_v, in_sem.at[1])
    c_n = pltpu.make_async_copy(nbr_hbm, n_v, in_sem.at[2])
    c_w = pltpu.make_async_copy(w_hbm, w_v, in_sem.at[3])
    c_l = pltpu.make_async_copy(send_hbm, l_v, in_sem.at[4])
    c_d.start()
    c_s.start()
    c_w.start()
    c_l.start()
    c_n.start()

    barrier = pltpu.get_barrier_semaphore()
    for k in range(1, n):
        pl.semaphore_signal(barrier, inc=1, device_id={"cell": (cell + k) % n}, device_id_type=MESH)
    pl.semaphore_signal(barrier, inc=1, device_id={"dp": sibling}, device_id_type=MESH)
    for k in range(1, n_y):
        pl.semaphore_signal(
            barrier, inc=1, device_id={"dp": ((y + k) % n_y) * 2 + core}, device_id_type=MESH
        )

    count = cnt_ref[0]
    live = lax.broadcasted_iota(jnp.int32, (1, slots), 1) < count
    c_d.wait()
    masked = jnp.where(live, d_v[...].astype(F32), F32(0.0))
    pmf[...] = masked
    c_s.wait()
    preds[cell] = lax.dot_general(
        masked.astype(BF16), s_v[...], (((1,), (1,)), ((), ())), preferred_element_type=F32
    )

    pl.semaphore_wait(barrier, n + n_y - 1)
    sends = []
    for k in range(1, n):
        copy = pltpu.make_async_remote_copy(
            src_ref=preds.at[cell], dst_ref=preds.at[cell],
            send_sem=bar_pred_s.at[k], recv_sem=bar_pred_r.at[cell],
            device_id={"cell": (cell + k) % n}, device_id_type=MESH,
        )
        copy.start()
        sends.append(copy)

    c_w.wait()
    for j in range(nb):
        wrow[:, j * LANES : (j + 1) * LANES] = w_v[j : j + 1, :]
    weight = jnp.where(live, wrow[...], F32(0.0))
    wrow[...] = weight

    pad = jnp.zeros((nvec, LANES), F32)
    wide = jnp.concatenate([masked * weight, pad], axis=1)
    wide_w = jnp.concatenate([weight, pad[:1]], axis=1)
    wide_w = pltpu.roll(jnp.broadcast_to(wide_w, (8, slots + LANES)), REACH, 1)
    g[...] = stack_rows(pltpu.roll(wide, REACH, 1), wide_w[0:1])

    c_l.wait()
    lists = jnp.concatenate([l_v[0, 0:1, :], l_v[0, 1:2, :]], axis=1) + REACH
    step = 10 * LANES if (slots + LANES) % (10 * LANES) == 0 else LANES

    def pick(i, total):
        at = pl.multiple_of(i * step, step)
        hits = count_hits(lists - at, step)
        return total + jnp.dot(g[:, pl.ds(at, step)], hits, preferred_element_type=F32)

    picked = lax.fori_loop(
        0, (slots + LANES) // step, pick, jnp.zeros((3 * nvec, 2 * rim), F32)
    )
    for side in range(2):
        part = picked[:, side * rim : (side + 1) * rim]
        rim_out[side, 0:16] = part[0:16] + part[16:32]
        rim_out[side, 16:24] = jnp.broadcast_to(part[32:33] + part[33:34], (8, rim))
    for side in range(2):
        copy = pltpu.make_async_remote_copy(
            src_ref=rim_out.at[side], dst_ref=rim_in.at[1 - side],
            send_sem=rim_s.at[side], recv_sem=rim_r.at[1 - side],
            device_id={"cell": (cell + n - 1 + 2 * side) % n}, device_id_type=MESH,
        )
        copy.start()
        sends.append(copy)

    first_t = jnp.minimum(y * piece, half - piece)
    first_block = first_t + core * (nb - 2 * first_t - piece)
    sm[...] = jnp.zeros_like(sm)
    c_n.wait()

    def near(i, carry):
        at = pl.multiple_of((first_block + i) * LANES, LANES)
        hits = count_hits(n_v[:, pl.ds(at, LANES)] - at + REACH, 2 * LANES)
        acc[i] = jnp.dot(g[:, pl.ds(at, 2 * LANES)], hits, preferred_element_type=F32)
        return carry

    lax.fori_loop(0, piece, near, 0, unroll=True)

    sides = []
    for side in range(2):
        pltpu.make_async_remote_copy(
            src_ref=rim_out.at[side], dst_ref=rim_in.at[side],
            send_sem=rim_s.at[side], recv_sem=rim_r.at[side],
            device_id={"cell": (cell + n - 1 + 2 * side) % n}, device_id_type=MESH,
        ).wait_recv()
        there = cell > 0 if side == 0 else cell < n - 1
        got = jnp.where(there, rim_in[side], F32(0.0))
        sides.append(stack_rows(got[0:16], got[16:17]))
    rim_rows = jnp.concatenate(sides, axis=1)

    def far(i, carry):
        block = first_block + i
        at = pl.multiple_of(block * LANES, LANES)
        hits = count_hits(n_v[:, pl.ds(at, LANES)] - slots, 2 * rim)
        found = acc[i] + jnp.dot(rim_rows, hits, preferred_element_type=F32)
        sum_pw = found[0:16] + found[16:32]
        sum_w = found[32:33] + found[33:34]
        own_p = pmf[:, pl.ds(at, LANES)]
        own_w = wrow[:, pl.ds(at, LANES)]
        smooth = own_w * own_w * own_p + own_w * (own_p * sum_w - sum_pw)
        t = block + core * (nb - 1 - 2 * block)
        mine = jnp.logical_and(t >= y * piece, t < (y + 1) * piece)
        sm[:, pl.ds(at, LANES)] = smooth * jnp.where(mine, F32(0.5), F32(0.0))
        return carry

    lax.fori_loop(0, piece, far, 0, unroll=True)

    for k in range(1, n):
        source = (cell + k) % n
        pltpu.make_async_remote_copy(
            src_ref=preds.at[source], dst_ref=preds.at[source],
            send_sem=bar_pred_s.at[k], recv_sem=bar_pred_r.at[source],
            device_id={"cell": source}, device_id_type=MESH,
        ).wait_recv()
    predicted = preds[0]
    for k in range(1, n):
        predicted = predicted + preds[k]
    stacked = jnp.concatenate(split2(predicted), axis=0)

    def misfit(at):
        both = jnp.dot(stacked, s_v[:, pl.ds(at, chunk * LANES)], preferred_element_type=F32)
        return both[:nvec] + both[nvec:]

    def lanes_at(block):
        return pl.multiple_of(block * LANES, LANES)

    for c in range(n_chunks):
        a, b = c * chunk, (c + 1) * chunk
        ms[c] = misfit(lanes_at((1 - core) * (nb - b) + core * a))
        copy = pltpu.make_async_remote_copy(
            src_ref=ms.at[c], dst_ref=rs.at[c], send_sem=rs_s.at[c], recv_sem=rs_r.at[c],
            device_id={"dp": sibling}, device_id_type=MESH,
        )
        copy.start()
        sends.append(copy)

    for c in range(n_chunks):
        a, b = c * chunk, (c + 1) * chunk
        at = lanes_at(core * (nb - b) + (1 - core) * a)
        own = misfit(at)
        pltpu.make_async_remote_copy(
            src_ref=ms.at[c], dst_ref=rs.at[c], send_sem=rs_s.at[c], recv_sem=rs_r.at[c],
            device_id={"dp": sibling}, device_id_type=MESH,
        ).wait_recv()
        ys[y, c] = (own + rs[c]) + sm[:, pl.ds(at, chunk * LANES)]
        for k in range(1, n_y):
            copy = pltpu.make_async_remote_copy(
                src_ref=ys.at[y, c], dst_ref=ys.at[y, c],
                send_sem=y_s.at[k, c], recv_sem=y_r.at[y, c],
                device_id={"dp": ((y + k) % n_y) * 2 + core}, device_id_type=MESH,
            )
            copy.start()
            sends.append(copy)

    final = []
    for c in range(n_chunks):
        a, b = c * chunk, (c + 1) * chunk
        at = lanes_at(core * (nb - b) + (1 - core) * a)
        for k in range(1, n_y):
            source = (y + k) % n_y
            pltpu.make_async_remote_copy(
                src_ref=ys.at[source, c], dst_ref=ys.at[source, c],
                send_sem=y_s.at[k, c], recv_sem=y_r.at[source, c],
                device_id={"dp": source * 2 + core}, device_id_type=MESH,
            ).wait_recv()
        total = ys[0, c]
        for k in range(1, n_y):
            total = total + ys[k, c]
        place = lax.broadcasted_iota(jnp.int32, (1, chunk * LANES), 1) + at
        out_ref[:, pl.ds(at, chunk * LANES)] = jnp.where(place < count, total, F32(0.0))
        end = min(b, swap_end)
        if end > a:
            width = (end - a) * LANES
            here = lanes_at(core * (nb - end) + (1 - core) * a)
            there = lanes_at((1 - core) * (nb - end) + core * a)
            copy = pltpu.make_async_remote_copy(
                src_ref=out_ref.at[:, pl.ds(here, width)], dst_ref=out_ref.at[:, pl.ds(here, width)],
                send_sem=fin_s.at[c], recv_sem=fin_r.at[c],
                device_id={"dp": sibling}, device_id_type=MESH,
            )
            copy.start()
            sends.append(copy)
            final.append(
                pltpu.make_async_remote_copy(
                    src_ref=out_ref.at[:, pl.ds(there, width)],
                    dst_ref=out_ref.at[:, pl.ds(there, width)],
                    send_sem=fin_s.at[c], recv_sem=fin_r.at[c],
                    device_id={"dp": sibling}, device_id_type=MESH,
                )
            )
    for copy in final:
        copy.wait_recv()
    for copy in sends:
        copy.wait_send()


def on_device(n, n_dp, sensitivity, direction, depth_weight, counts, send_lists, neighbours):
    ndata, slots = sensitivity.shape
    nvec = direction.shape[0]
    faces = neighbours.shape[0]
    rim = send_lists.shape[2]
    nb = slots // LANES
    half = (nb + 1) // 2
    chunk = pick_chunk(half)
    n_chunks = half // chunk
    n_y = n_dp // 2
    piece = (half + n_y - 1) // n_y
    vmem = pl.BlockSpec(memory_space=pltpu.VMEM)
    hbm = pl.BlockSpec(memory_space=pltpu.HBM)
    dma = pltpu.SemaphoreType.DMA
    return pl.pallas_call(
        functools.partial(kernel, n, n_dp),
        out_shape=jax.ShapeDtypeStruct((nvec, slots), F32),
        in_specs=[hbm, hbm, hbm, pl.BlockSpec(memory_space=pltpu.SMEM), hbm, hbm],
        out_specs=vmem,
        scratch_shapes=[
            pltpu.VMEM((ndata, slots), BF16),
            pltpu.VMEM((nvec, slots), BF16),
            pltpu.VMEM((faces, slots), jnp.int32),
            pltpu.VMEM((nb, LANES), F32),
            pltpu.VMEM(send_lists.shape, jnp.int32),
            pltpu.VMEM((3 * nvec, slots + LANES), BF16),
            pltpu.VMEM((nvec, slots), F32),
            pltpu.VMEM((1, slots), F32),
            pltpu.VMEM((n, nvec, ndata), F32),
            pltpu.VMEM((2, nvec + 8, rim), F32),
            pltpu.VMEM((2, nvec + 8, rim), F32),
            pltpu.VMEM((piece, 3 * nvec, LANES), F32),
            pltpu.VMEM((nvec, slots), F32),
            pltpu.VMEM((n_chunks, nvec, chunk * LANES), F32),
            pltpu.VMEM((n_chunks, nvec, chunk * LANES), F32),
            pltpu.VMEM((n_y, n_chunks, nvec, chunk * LANES), F32),
            dma((5,)),
            dma((n,)),
            dma((n,)),
            dma((2,)),
            dma((2,)),
            dma((n_chunks,)),
            dma((n_chunks,)),
            dma((n_y, n_chunks)),
            dma((n_y, n_chunks)),
            dma((n_chunks,)),
            dma((n_chunks,)),
        ],
        compiler_params=pltpu.CompilerParams(
            collective_id=0, has_side_effects=True, vmem_limit_bytes=64000 * 1024
        ),
    )(sensitivity, direction, depth_weight.reshape(nb, LANES), counts, send_lists, neighbours)


def solution(mesh):
    placed = (
        P("dp", "cell"),
        P(None, "cell"),
        P("cell"),
        P("cell"),
        P("cell", None, None),
        P(None, "cell"),
    )
    return jax.shard_map(
        functools.partial(on_device, mesh.shape["cell"], mesh.shape["dp"]),
        mesh=mesh, in_specs=placed, out_specs=P(None, "cell"), check_vma=False,
    )
```

```python
import functools

import jax
import jax.numpy as jnp
from jax import lax
from jax.experimental import pallas as pl
from jax.experimental.pallas import tpu as pltpu
from jax.sharding import PartitionSpec as P

LANES = 128
REACH = 64
MESH = pl.DeviceIdType.MESH
F32 = jnp.float32
BF16 = jnp.bfloat16


def pick_chunk(blocks):
    for size in (5, 6, 4, 3, 2):
        if blocks % size == 0:
            return size
    return 1


def split2(value):
    hi = value.astype(BF16)
    return hi, (value - hi.astype(F32)).astype(BF16)


def stack_rows(weighted, weight):
    hi, lo = split2(weighted)
    w_hi, w_lo = split2(weight)
    shape = (16, weight.shape[1])
    row = lax.broadcasted_iota(jnp.int32, shape, 0)
    wide_hi = jnp.broadcast_to(w_hi.astype(F32), shape)
    wide_lo = jnp.broadcast_to(w_lo.astype(F32), shape)
    tail = jnp.where(row == 0, wide_hi, jnp.where(row == 1, wide_lo, F32(0.0)))
    return jnp.concatenate([hi, lo, tail.astype(BF16)], axis=0)


def count_hits(columns, rows):
    narrow = columns.astype(jnp.int16)
    target = lax.broadcasted_iota(jnp.int16, (rows, columns.shape[1]), 0)
    hits = jnp.zeros((rows, columns.shape[1]), BF16)
    for k in range(columns.shape[0]):
        hits = hits + jnp.where(narrow[k : k + 1, :] == target, BF16(1.0), BF16(0.0))
    return hits


def kernel(
    n, n_dp, sens_hbm, dir_hbm, w_hbm, cnt_ref, send_hbm, nbr_hbm, out_ref,
    s_v, d_v, n_v, w_v, l_v, g, pmf, wrow, preds, rim_out, rim_in, acc, sm, ms, rs, ys,
    in_sem, bar_pred_s, bar_pred_r, rim_s, rim_r, rs_s, rs_r, y_s, y_r, fin_s, fin_r,
):
    nvec, slots = d_v.shape
    nb = slots // LANES
    half = (nb + 1) // 2
    swap_end = nb - half
    chunk = pick_chunk(half)
    n_chunks = half // chunk
    n_y = n_dp // 2
    piece = (half + n_y - 1) // n_y
    rim = rim_out.shape[2]

    cell = lax.axis_index("cell")
    dp = lax.axis_index("dp")
    y = dp // 2
    core = dp % 2
    sibling = y * 2 + 1 - core

    c_s = pltpu.make_async_copy(sens_hbm, s_v, in_sem.at[0])
    c_d = pltpu.make_async_copy(dir_hbm, d_v, in_sem.at[1])
    c_n = pltpu.make_async_copy(nbr_hbm, n_v, in_sem.at[2])
    c_w = pltpu.make_async_copy(w_hbm, w_v, in_sem.at[3])
    c_l = pltpu.make_async_copy(send_hbm, l_v, in_sem.at[4])
    c_d.start()
    c_s.start()
    c_w.start()
    c_l.start()
    c_n.start()

    barrier = pltpu.get_barrier_semaphore()
    for k in range(1, n):
        pl.semaphore_signal(barrier, inc=1, device_id={"cell": (cell + k) % n}, device_id_type=MESH)
    pl.semaphore_signal(barrier, inc=1, device_id={"dp": sibling}, device_id_type=MESH)
    for k in range(1, n_y):
        pl.semaphore_signal(
            barrier, inc=1, device_id={"dp": ((y + k) % n_y) * 2 + core}, device_id_type=MESH
        )

    count = cnt_ref[0]
    live = lax.broadcasted_iota(jnp.int32, (1, slots), 1) < count
    c_d.wait()
    masked = jnp.where(live, d_v[...].astype(F32), F32(0.0))
    pmf[...] = masked
    c_s.wait()
    preds[cell] = lax.dot_general(
        masked.astype(BF16), s_v[...], (((1,), (1,)), ((), ())), preferred_element_type=F32
    )

    pl.semaphore_wait(barrier, n + n_y - 1)
    sends = []
    for k in range(1, n):
        copy = pltpu.make_async_remote_copy(
            src_ref=preds.at[cell], dst_ref=preds.at[cell],
            send_sem=bar_pred_s.at[k], recv_sem=bar_pred_r.at[cell],
            device_id={"cell": (cell + k) % n}, device_id_type=MESH,
        )
        copy.start()
        sends.append(copy)

    c_w.wait()
    for j in range(nb):
        wrow[:, j * LANES : (j + 1) * LANES] = w_v[j : j + 1, :]
    weight = jnp.where(live, wrow[...], F32(0.0))
    wrow[...] = weight

    pad = jnp.zeros((nvec, LANES), F32)
    wide = jnp.concatenate([masked * weight, pad], axis=1)
    wide_w = jnp.concatenate([weight, pad[:1]], axis=1)
    wide_w = pltpu.roll(jnp.broadcast_to(wide_w, (8, slots + LANES)), REACH, 1)
    g[...] = stack_rows(pltpu.roll(wide, REACH, 1), wide_w[0:1])

    c_l.wait()
    lists = jnp.concatenate([l_v[0, 0:1, :], l_v[0, 1:2, :]], axis=1) + REACH
    step = 10 * LANES if (slots + LANES) % (10 * LANES) == 0 else LANES

    def pick(i, total):
        at = pl.multiple_of(i * step, step)
        hits = count_hits(lists - at, step)
        return total + jnp.dot(g[:, pl.ds(at, step)], hits, preferred_element_type=F32)

    picked = lax.fori_loop(
        0, (slots + LANES) // step, pick, jnp.zeros((3 * nvec, 2 * rim), F32), unroll=True
    )
    for side in range(2):
        part = picked[:, side * rim : (side + 1) * rim]
        rim_out[side, 0:16] = part[0:16] + part[16:32]
        rim_out[side, 16:24] = jnp.broadcast_to(part[32:33] + part[33:34], (8, rim))
    for side in range(2):
        copy = pltpu.make_async_remote_copy(
            src_ref=rim_out.at[side], dst_ref=rim_in.at[1 - side],
            send_sem=rim_s.at[side], recv_sem=rim_r.at[1 - side],
            device_id={"cell": (cell + n - 1 + 2 * side) % n}, device_id_type=MESH,
        )
        copy.start()
        sends.append(copy)

    first_t = jnp.minimum(y * piece, half - piece)
    first_block = first_t + core * (nb - 2 * first_t - piece)
    sm[...] = jnp.zeros_like(sm)
    c_n.wait()

    def near(i, carry):
        at = pl.multiple_of((first_block + i) * LANES, LANES)
        hits = count_hits(n_v[:, pl.ds(at, LANES)] - at + REACH, 2 * LANES)
        acc[i] = jnp.dot(g[:, pl.ds(at, 2 * LANES)], hits, preferred_element_type=F32)
        return carry

    lax.fori_loop(0, piece, near, 0, unroll=True)

    sides = []
    for side in range(2):
        pltpu.make_async_remote_copy(
            src_ref=rim_out.at[side], dst_ref=rim_in.at[side],
            send_sem=rim_s.at[side], recv_sem=rim_r.at[side],
            device_id={"cell": (cell + n - 1 + 2 * side) % n}, device_id_type=MESH,
        ).wait_recv()
        there = cell > 0 if side == 0 else cell < n - 1
        got = jnp.where(there, rim_in[side], F32(0.0))
        sides.append(stack_rows(got[0:16], got[16:17]))
    rim_rows = jnp.concatenate(sides, axis=1)

    def far(i, carry):
        block = first_block + i
        at = pl.multiple_of(block * LANES, LANES)
        hits = count_hits(n_v[:, pl.ds(at, LANES)] - slots, 2 * rim)
        found = acc[i] + jnp.dot(rim_rows, hits, preferred_element_type=F32)
        sum_pw = found[0:16] + found[16:32]
        sum_w = found[32:33] + found[33:34]
        own_p = pmf[:, pl.ds(at, LANES)]
        own_w = wrow[:, pl.ds(at, LANES)]
        smooth = own_w * own_w * own_p + own_w * (own_p * sum_w - sum_pw)
        t = block + core * (nb - 1 - 2 * block)
        mine = jnp.logical_and(t >= y * piece, t < (y + 1) * piece)
        sm[:, pl.ds(at, LANES)] = smooth * jnp.where(mine, F32(0.5), F32(0.0))
        return carry

    lax.fori_loop(0, piece, far, 0, unroll=True)

    for k in range(1, n):
        source = (cell + k) % n
        pltpu.make_async_remote_copy(
            src_ref=preds.at[source], dst_ref=preds.at[source],
            send_sem=bar_pred_s.at[k], recv_sem=bar_pred_r.at[source],
            device_id={"cell": source}, device_id_type=MESH,
        ).wait_recv()
    predicted = preds[0]
    for k in range(1, n):
        predicted = predicted + preds[k]
    stacked = jnp.concatenate(split2(predicted), axis=0)

    def misfit(at):
        both = jnp.dot(stacked, s_v[:, pl.ds(at, chunk * LANES)], preferred_element_type=F32)
        return both[:nvec] + both[nvec:]

    def lanes_at(block):
        return pl.multiple_of(block * LANES, LANES)

    for c in range(n_chunks):
        a, b = c * chunk, (c + 1) * chunk
        ms[c] = misfit(lanes_at((1 - core) * (nb - b) + core * a))
        copy = pltpu.make_async_remote_copy(
            src_ref=ms.at[c], dst_ref=rs.at[c], send_sem=rs_s.at[c], recv_sem=rs_r.at[c],
            device_id={"dp": sibling}, device_id_type=MESH,
        )
        copy.start()
        sends.append(copy)

    for c in range(n_chunks):
        a, b = c * chunk, (c + 1) * chunk
        at = lanes_at(core * (nb - b) + (1 - core) * a)
        own = misfit(at)
        pltpu.make_async_remote_copy(
            src_ref=ms.at[c], dst_ref=rs.at[c], send_sem=rs_s.at[c], recv_sem=rs_r.at[c],
            device_id={"dp": sibling}, device_id_type=MESH,
        ).wait_recv()
        ys[y, c] = (own + rs[c]) + sm[:, pl.ds(at, chunk * LANES)]
        for k in range(1, n_y):
            copy = pltpu.make_async_remote_copy(
                src_ref=ys.at[y, c], dst_ref=ys.at[y, c],
                send_sem=y_s.at[k, c], recv_sem=y_r.at[y, c],
                device_id={"dp": ((y + k) % n_y) * 2 + core}, device_id_type=MESH,
            )
            copy.start()
            sends.append(copy)

    final = []
    for c in range(n_chunks):
        a, b = c * chunk, (c + 1) * chunk
        at = lanes_at(core * (nb - b) + (1 - core) * a)
        for k in range(1, n_y):
            source = (y + k) % n_y
            pltpu.make_async_remote_copy(
                src_ref=ys.at[source, c], dst_ref=ys.at[source, c],
                send_sem=y_s.at[k, c], recv_sem=y_r.at[source, c],
                device_id={"dp": source * 2 + core}, device_id_type=MESH,
            ).wait_recv()
        total = ys[0, c]
        for k in range(1, n_y):
            total = total + ys[k, c]
        place = lax.broadcasted_iota(jnp.int32, (1, chunk * LANES), 1) + at
        out_ref[:, pl.ds(at, chunk * LANES)] = jnp.where(place < count, total, F32(0.0))
        end = min(b, swap_end)
        if end > a:
            width = (end - a) * LANES
            here = lanes_at(core * (nb - end) + (1 - core) * a)
            there = lanes_at((1 - core) * (nb - end) + core * a)
            copy = pltpu.make_async_remote_copy(
                src_ref=out_ref.at[:, pl.ds(here, width)], dst_ref=out_ref.at[:, pl.ds(here, width)],
                send_sem=fin_s.at[c], recv_sem=fin_r.at[c],
                device_id={"dp": sibling}, device_id_type=MESH,
            )
            copy.start()
            sends.append(copy)
            final.append(
                pltpu.make_async_remote_copy(
                    src_ref=out_ref.at[:, pl.ds(there, width)],
                    dst_ref=out_ref.at[:, pl.ds(there, width)],
                    send_sem=fin_s.at[c], recv_sem=fin_r.at[c],
                    device_id={"dp": sibling}, device_id_type=MESH,
                )
            )
    for copy in final:
        copy.wait_recv()
    for copy in sends:
        copy.wait_send()


def on_device(n, n_dp, sensitivity, direction, depth_weight, counts, send_lists, neighbours):
    ndata, slots = sensitivity.shape
    nvec = direction.shape[0]
    faces = neighbours.shape[0]
    rim = send_lists.shape[2]
    nb = slots // LANES
    half = (nb + 1) // 2
    chunk = pick_chunk(half)
    n_chunks = half // chunk
    n_y = n_dp // 2
    piece = (half + n_y - 1) // n_y
    vmem = pl.BlockSpec(memory_space=pltpu.VMEM)
    hbm = pl.BlockSpec(memory_space=pltpu.HBM)
    dma = pltpu.SemaphoreType.DMA
    return pl.pallas_call(
        functools.partial(kernel, n, n_dp),
        out_shape=jax.ShapeDtypeStruct((nvec, slots), F32),
        in_specs=[hbm, hbm, hbm, pl.BlockSpec(memory_space=pltpu.SMEM), hbm, hbm],
        out_specs=vmem,
        scratch_shapes=[
            pltpu.VMEM((ndata, slots), BF16),
            pltpu.VMEM((nvec, slots), BF16),
            pltpu.VMEM((faces, slots), jnp.int32),
            pltpu.VMEM((nb, LANES), F32),
            pltpu.VMEM(send_lists.shape, jnp.int32),
            pltpu.VMEM((3 * nvec, slots + LANES), BF16),
            pltpu.VMEM((nvec, slots), F32),
            pltpu.VMEM((1, slots), F32),
            pltpu.VMEM((n, nvec, ndata), F32),
            pltpu.VMEM((2, nvec + 8, rim), F32),
            pltpu.VMEM((2, nvec + 8, rim), F32),
            pltpu.VMEM((piece, 3 * nvec, LANES), F32),
            pltpu.VMEM((nvec, slots), F32),
            pltpu.VMEM((n_chunks, nvec, chunk * LANES), F32),
            pltpu.VMEM((n_chunks, nvec, chunk * LANES), F32),
            pltpu.VMEM((n_y, n_chunks, nvec, chunk * LANES), F32),
            dma((5,)),
            dma((n,)),
            dma((n,)),
            dma((2,)),
            dma((2,)),
            dma((n_chunks,)),
            dma((n_chunks,)),
            dma((n_y, n_chunks)),
            dma((n_y, n_chunks)),
            dma((n_chunks,)),
            dma((n_chunks,)),
        ],
        compiler_params=pltpu.CompilerParams(
            collective_id=0, has_side_effects=True, vmem_limit_bytes=64000 * 1024
        ),
    )(sensitivity, direction, depth_weight.reshape(nb, LANES), counts, send_lists, neighbours)


def solution(mesh):
    placed = (
        P("dp", "cell"),
        P(None, "cell"),
        P("cell"),
        P("cell"),
        P("cell", None, None),
        P(None, "cell"),
    )
    return jax.shard_map(
        functools.partial(on_device, mesh.shape["cell"], mesh.shape["dp"]),
        mesh=mesh, in_specs=placed, out_specs=P(None, "cell"), check_vma=False,
    )
```

```python
import functools

import jax
import jax.numpy as jnp
from jax import lax
from jax.experimental import pallas as pl
from jax.experimental.pallas import tpu as pltpu
from jax.sharding import PartitionSpec as P

LANES = 128
REACH = 64
MESH = pl.DeviceIdType.MESH
F32 = jnp.float32
BF16 = jnp.bfloat16


def pick_chunk(blocks):
    for size in (5, 6, 4, 3, 2):
        if blocks % size == 0:
            return size
    return 1


def split2(value):
    hi = value.astype(BF16)
    return hi, (value - hi.astype(F32)).astype(BF16)


def stack_rows(weighted, weight):
    hi, lo = split2(weighted)
    w_hi, w_lo = split2(weight)
    shape = (16, weight.shape[1])
    row = lax.broadcasted_iota(jnp.int32, shape, 0)
    wide_hi = jnp.broadcast_to(w_hi.astype(F32), shape)
    wide_lo = jnp.broadcast_to(w_lo.astype(F32), shape)
    tail = jnp.where(row == 0, wide_hi, jnp.where(row == 1, wide_lo, F32(0.0)))
    return jnp.concatenate([hi, lo, tail.astype(BF16)], axis=0)


def count_hits(columns, rows):
    narrow = columns.astype(jnp.int16)
    target = lax.broadcasted_iota(jnp.int16, (rows, columns.shape[1]), 0)
    hits = jnp.zeros((rows, columns.shape[1]), BF16)
    for k in range(columns.shape[0]):
        hits = hits + jnp.where(narrow[k : k + 1, :] == target, BF16(1.0), BF16(0.0))
    return hits


def kernel(
    n, n_dp, sens_hbm, dir_hbm, w_hbm, cnt_ref, send_hbm, nbr_hbm, out_hbm,
    s_v, d_v, n_v, w_v, l_v, g, pmf, wrow, preds, rim_out, rim_in, acc, sm, ms, rs, ys,
    in_sem, bar_pred_s, bar_pred_r, rim_s, rim_r, rs_s, rs_r, y_s, y_r, fin_s, fin_r, out_ref, o_s,
):
    nvec, slots = d_v.shape
    nb = slots // LANES
    half = (nb + 1) // 2
    swap_end = nb - half
    chunk = pick_chunk(half)
    n_chunks = half // chunk
    n_y = n_dp // 2
    piece = (half + n_y - 1) // n_y
    rim = rim_out.shape[2]

    cell = lax.axis_index("cell")
    dp = lax.axis_index("dp")
    y = dp // 2
    core = dp % 2
    sibling = y * 2 + 1 - core

    c_s = pltpu.make_async_copy(sens_hbm, s_v, in_sem.at[0])
    c_d = pltpu.make_async_copy(dir_hbm, d_v, in_sem.at[1])
    c_n = pltpu.make_async_copy(nbr_hbm, n_v, in_sem.at[2])
    c_w = pltpu.make_async_copy(w_hbm, w_v, in_sem.at[3])
    c_l = pltpu.make_async_copy(send_hbm, l_v, in_sem.at[4])
    c_d.start()
    c_s.start()
    c_w.start()
    c_l.start()
    c_n.start()

    barrier = pltpu.get_barrier_semaphore()
    for k in range(1, n):
        pl.semaphore_signal(barrier, inc=1, device_id={"cell": (cell + k) % n}, device_id_type=MESH)
    pl.semaphore_signal(barrier, inc=1, device_id={"dp": sibling}, device_id_type=MESH)
    for k in range(1, n_y):
        pl.semaphore_signal(
            barrier, inc=1, device_id={"dp": ((y + k) % n_y) * 2 + core}, device_id_type=MESH
        )

    count = cnt_ref[0]
    live = lax.broadcasted_iota(jnp.int32, (1, slots), 1) < count
    c_d.wait()
    masked = jnp.where(live, d_v[...].astype(F32), F32(0.0))
    pmf[...] = masked
    c_s.wait()
    preds[cell] = lax.dot_general(
        masked.astype(BF16), s_v[...], (((1,), (1,)), ((), ())), preferred_element_type=F32
    )

    pl.semaphore_wait(barrier, n + n_y - 1)
    sends = []
    for k in range(1, n):
        copy = pltpu.make_async_remote_copy(
            src_ref=preds.at[cell], dst_ref=preds.at[cell],
            send_sem=bar_pred_s.at[k], recv_sem=bar_pred_r.at[cell],
            device_id={"cell": (cell + k) % n}, device_id_type=MESH,
        )
        copy.start()
        sends.append(copy)

    c_w.wait()
    for j in range(nb):
        wrow[:, j * LANES : (j + 1) * LANES] = w_v[j : j + 1, :]
    weight = jnp.where(live, wrow[...], F32(0.0))
    wrow[...] = weight

    pad = jnp.zeros((nvec, LANES), F32)
    wide = jnp.concatenate([masked * weight, pad], axis=1)
    wide_w = jnp.concatenate([weight, pad[:1]], axis=1)
    wide_w = pltpu.roll(jnp.broadcast_to(wide_w, (8, slots + LANES)), REACH, 1)
    g[...] = stack_rows(pltpu.roll(wide, REACH, 1), wide_w[0:1])

    c_l.wait()
    lists = jnp.concatenate([l_v[0, 0:1, :], l_v[0, 1:2, :]], axis=1) + REACH
    step = 10 * LANES if (slots + LANES) % (10 * LANES) == 0 else LANES

    def pick(i, total):
        at = pl.multiple_of(i * step, step)
        hits = count_hits(lists - at, step)
        return total + jnp.dot(g[:, pl.ds(at, step)], hits, preferred_element_type=F32)

    picked = lax.fori_loop(
        0, (slots + LANES) // step, pick, jnp.zeros((3 * nvec, 2 * rim), F32)
    )
    for side in range(2):
        part = picked[:, side * rim : (side + 1) * rim]
        rim_out[side, 0:16] = part[0:16] + part[16:32]
        rim_out[side, 16:24] = jnp.broadcast_to(part[32:33] + part[33:34], (8, rim))
    for side in range(2):
        copy = pltpu.make_async_remote_copy(
            src_ref=rim_out.at[side], dst_ref=rim_in.at[1 - side],
            send_sem=rim_s.at[side], recv_sem=rim_r.at[1 - side],
            device_id={"cell": (cell + n - 1 + 2 * side) % n}, device_id_type=MESH,
        )
        copy.start()
        sends.append(copy)

    first_t = jnp.minimum(y * piece, half - piece)
    first_block = first_t + core * (nb - 2 * first_t - piece)
    sm[...] = jnp.zeros_like(sm)
    c_n.wait()

    def near(i, carry):
        at = pl.multiple_of((first_block + i) * LANES, LANES)
        hits = count_hits(n_v[:, pl.ds(at, LANES)] - at + REACH, 2 * LANES)
        acc[i] = jnp.dot(g[:, pl.ds(at, 2 * LANES)], hits, preferred_element_type=F32)
        return carry

    lax.fori_loop(0, piece, near, 0, unroll=True)

    sides = []
    for side in range(2):
        pltpu.make_async_remote_copy(
            src_ref=rim_out.at[side], dst_ref=rim_in.at[side],
            send_sem=rim_s.at[side], recv_sem=rim_r.at[side],
            device_id={"cell": (cell + n - 1 + 2 * side) % n}, device_id_type=MESH,
        ).wait_recv()
        there = cell > 0 if side == 0 else cell < n - 1
        got = jnp.where(there, rim_in[side], F32(0.0))
        sides.append(stack_rows(got[0:16], got[16:17]))
    rim_rows = jnp.concatenate(sides, axis=1)

    def far(i, carry):
        block = first_block + i
        at = pl.multiple_of(block * LANES, LANES)
        hits = count_hits(n_v[:, pl.ds(at, LANES)] - slots, 2 * rim)
        found = acc[i] + jnp.dot(rim_rows, hits, preferred_element_type=F32)
        sum_pw = found[0:16] + found[16:32]
        sum_w = found[32:33] + found[33:34]
        own_p = pmf[:, pl.ds(at, LANES)]
        own_w = wrow[:, pl.ds(at, LANES)]
        smooth = own_w * own_w * own_p + own_w * (own_p * sum_w - sum_pw)
        t = block + core * (nb - 1 - 2 * block)
        mine = jnp.logical_and(t >= y * piece, t < (y + 1) * piece)
        sm[:, pl.ds(at, LANES)] = smooth * jnp.where(mine, F32(0.5), F32(0.0))
        return carry

    lax.fori_loop(0, piece, far, 0, unroll=True)

    for k in range(1, n):
        source = (cell + k) % n
        pltpu.make_async_remote_copy(
            src_ref=preds.at[source], dst_ref=preds.at[source],
            send_sem=bar_pred_s.at[k], recv_sem=bar_pred_r.at[source],
            device_id={"cell": source}, device_id_type=MESH,
        ).wait_recv()
    predicted = preds[0]
    for k in range(1, n):
        predicted = predicted + preds[k]
    stacked = jnp.concatenate(split2(predicted), axis=0)

    def misfit(at):
        both = jnp.dot(stacked, s_v[:, pl.ds(at, chunk * LANES)], preferred_element_type=F32)
        return both[:nvec] + both[nvec:]

    def lanes_at(block):
        return pl.multiple_of(block * LANES, LANES)

    for c in range(n_chunks):
        a, b = c * chunk, (c + 1) * chunk
        ms[c] = misfit(lanes_at((1 - core) * (nb - b) + core * a))
        copy = pltpu.make_async_remote_copy(
            src_ref=ms.at[c], dst_ref=rs.at[c], send_sem=rs_s.at[c], recv_sem=rs_r.at[c],
            device_id={"dp": sibling}, device_id_type=MESH,
        )
        copy.start()
        sends.append(copy)

    for c in range(n_chunks):
        a, b = c * chunk, (c + 1) * chunk
        at = lanes_at(core * (nb - b) + (1 - core) * a)
        own = misfit(at)
        pltpu.make_async_remote_copy(
            src_ref=ms.at[c], dst_ref=rs.at[c], send_sem=rs_s.at[c], recv_sem=rs_r.at[c],
            device_id={"dp": sibling}, device_id_type=MESH,
        ).wait_recv()
        ys[y, c] = (own + rs[c]) + sm[:, pl.ds(at, chunk * LANES)]
        for k in range(1, n_y):
            copy = pltpu.make_async_remote_copy(
                src_ref=ys.at[y, c], dst_ref=ys.at[y, c],
                send_sem=y_s.at[k, c], recv_sem=y_r.at[y, c],
                device_id={"dp": ((y + k) % n_y) * 2 + core}, device_id_type=MESH,
            )
            copy.start()
            sends.append(copy)

    def write_back(block, width, slot):
        part = pl.ds(lanes_at(block), width)
        copy = pltpu.make_async_copy(out_ref.at[:, part], out_hbm.at[:, part], o_s.at[slot])
        copy.start()
        return copy

    final = []
    writes = []
    for c in range(n_chunks):
        a, b = c * chunk, (c + 1) * chunk
        at = lanes_at(core * (nb - b) + (1 - core) * a)
        for k in range(1, n_y):
            source = (y + k) % n_y
            pltpu.make_async_remote_copy(
                src_ref=ys.at[source, c], dst_ref=ys.at[source, c],
                send_sem=y_s.at[k, c], recv_sem=y_r.at[source, c],
                device_id={"dp": source * 2 + core}, device_id_type=MESH,
            ).wait_recv()
        total = ys[0, c]
        for k in range(1, n_y):
            total = total + ys[k, c]
        place = lax.broadcasted_iota(jnp.int32, (1, chunk * LANES), 1) + at
        out_ref[:, pl.ds(at, chunk * LANES)] = jnp.where(place < count, total, F32(0.0))
        writes.append(
            write_back(core * (nb - b) + (1 - core) * a, chunk * LANES, c)
        )
        end = min(b, swap_end)
        if end > a:
            width = (end - a) * LANES
            here = lanes_at(core * (nb - end) + (1 - core) * a)
            there = lanes_at((1 - core) * (nb - end) + core * a)
            copy = pltpu.make_async_remote_copy(
                src_ref=out_ref.at[:, pl.ds(here, width)], dst_ref=out_ref.at[:, pl.ds(here, width)],
                send_sem=fin_s.at[c], recv_sem=fin_r.at[c],
                device_id={"dp": sibling}, device_id_type=MESH,
            )
            copy.start()
            sends.append(copy)
            final.append((
                (1 - core) * (nb - end) + core * a, width, n_chunks + c,
                pltpu.make_async_remote_copy(
                    src_ref=out_ref.at[:, pl.ds(there, width)],
                    dst_ref=out_ref.at[:, pl.ds(there, width)],
                    send_sem=fin_s.at[c], recv_sem=fin_r.at[c],
                    device_id={"dp": sibling}, device_id_type=MESH,
                ),
            ))
    for block, width, slot, copy in final:
        copy.wait_recv()
        writes.append(write_back(block, width, slot))
    for copy in writes:
        copy.wait()
    for copy in sends:
        copy.wait_send()


def on_device(n, n_dp, sensitivity, direction, depth_weight, counts, send_lists, neighbours):
    ndata, slots = sensitivity.shape
    nvec = direction.shape[0]
    faces = neighbours.shape[0]
    rim = send_lists.shape[2]
    nb = slots // LANES
    half = (nb + 1) // 2
    chunk = pick_chunk(half)
    n_chunks = half // chunk
    n_y = n_dp // 2
    piece = (half + n_y - 1) // n_y
    vmem = pl.BlockSpec(memory_space=pltpu.VMEM)
    hbm = pl.BlockSpec(memory_space=pltpu.HBM)
    dma = pltpu.SemaphoreType.DMA
    return pl.pallas_call(
        functools.partial(kernel, n, n_dp),
        out_shape=jax.ShapeDtypeStruct((nvec, slots), F32),
        in_specs=[hbm, hbm, hbm, pl.BlockSpec(memory_space=pltpu.SMEM), hbm, hbm],
        out_specs=hbm,
        scratch_shapes=[
            pltpu.VMEM((ndata, slots), BF16),
            pltpu.VMEM((nvec, slots), BF16),
            pltpu.VMEM((faces, slots), jnp.int32),
            pltpu.VMEM((nb, LANES), F32),
            pltpu.VMEM(send_lists.shape, jnp.int32),
            pltpu.VMEM((3 * nvec, slots + LANES), BF16),
            pltpu.VMEM((nvec, slots), F32),
            pltpu.VMEM((1, slots), F32),
            pltpu.VMEM((n, nvec, ndata), F32),
            pltpu.VMEM((2, nvec + 8, rim), F32),
            pltpu.VMEM((2, nvec + 8, rim), F32),
            pltpu.VMEM((piece, 3 * nvec, LANES), F32),
            pltpu.VMEM((nvec, slots), F32),
            pltpu.VMEM((n_chunks, nvec, chunk * LANES), F32),
            pltpu.VMEM((n_chunks, nvec, chunk * LANES), F32),
            pltpu.VMEM((n_y, n_chunks, nvec, chunk * LANES), F32),
            dma((5,)),
            dma((n,)),
            dma((n,)),
            dma((2,)),
            dma((2,)),
            dma((n_chunks,)),
            dma((n_chunks,)),
            dma((n_y, n_chunks)),
            dma((n_y, n_chunks)),
            dma((n_chunks,)),
            dma((n_chunks,)),
            pltpu.VMEM((nvec, slots), F32),
            dma((2 * n_chunks,)),
        ],
        compiler_params=pltpu.CompilerParams(
            collective_id=0, has_side_effects=True, vmem_limit_bytes=64000 * 1024
        ),
    )(sensitivity, direction, depth_weight.reshape(nb, LANES), counts, send_lists, neighbours)


def solution(mesh):
    placed = (
        P("dp", "cell"),
        P(None, "cell"),
        P("cell"),
        P("cell"),
        P("cell", None, None),
        P(None, "cell"),
    )
    return jax.shard_map(
        functools.partial(on_device, mesh.shape["cell"], mesh.shape["dp"]),
        mesh=mesh, in_specs=placed, out_specs=P(None, "cell"), check_vma=False,
    )
```
